256 devices in a mesh: row: 8 (over z), col: 8 (over x, y_hi), rep: 4 (over y_lo, core).
Axes of the slice: x: 4, y: 4 (y_hi: 2, y_lo: 2; y = y_hi * 2 + y_lo), z: 8, core: 2. Of those that a mesh axis runs over, the one named last changes fastest.
Arguments:
- tokens_in: bfloat16 [1024, 12288], P(('col', 'rep'), 'row'), may hold values from -6 to 6
- w_up: bfloat16 [12288, 24576], P('row', ('col', 'rep')), may hold values from -0.0546875 to 0.0546875
- w_down: bfloat16 [24576, 12288], P(('col', 'rep'), 'row'), may hold values from -0.0390625 to 0.0390625
- grad_out: bfloat16 [1024, 12288], P(('col', 'rep'), 'row'), may hold values from -6 to 6
Outputs:
- output: bfloat16 [1024, 12288], P(('col', 'rep'), 'row')
- grad_tokens: bfloat16 [1024, 12288], P(('col', 'rep'), 'row')
- grad_w_up: bfloat16 [12288, 24576], P('row', ('col', 'rep'))
- grad_w_down: bfloat16 [24576, 12288], P(('col', 'rep'), 'row')
The draws below stay inside these ranges and needn't reach their ends.
All inputs are finite; a program needn't handle non-finite values.
Results may differ from the reference program's by a relative error of at most 0.0049.
Values may be sent and summed in bfloat16 or wider, within the bound.
No kernel may reach another device: no remote copies, remote signals or barrier semaphores. Data moves between devices by JAX's collectives and lax.ppermute only.
A program may use at most 128 MiB of HBM per device.

```python
import jax
import jax.numpy as jnp
from jax import lax

D = 12288
FF = 24576
TOK = 1024


def level_of(stream_key, dims, shards, low, top_value):
    def one(axis_at, shards_of):
        steps = jax.random.uniform(jax.random.fold_in(jax.random.fold_in(stream_key, 6), axis_at), (shards_of,), jnp.float32, low / len(shards), top_value / len(shards))
        return jnp.repeat(jnp.exp(steps), dims[axis_at] // shards_of).reshape((-1,) + (1,) * (len(dims) - axis_at - 1))

    level = one(*shards[0])
    for cut in shards[1:]:
        level = level * one(*cut)
    return level


def gaussian(own_key, dims, scale, most, split=(), kind=jnp.bfloat16):
    drawn = jax.random.normal(own_key, dims, jnp.float32) * scale
    if len(split) > 0:
        drawn = level_of(own_key, dims, split, -0.22, 0.18) * drawn
    return jnp.clip(drawn, min=-most, max=most).astype(kind)


def setup_inputs(seed: int = 0) -> dict:
    seeds = jax.random.split(jax.random.key(seed), 5)
    tokens_in = gaussian(seeds[0], (TOK, D), 1.0, 6.0, ((0, 32), (1, 8)))
    w_up = gaussian(seeds[1], (D, FF), D ** -0.5, 0.0546875, ((0, 8), (1, 32)))
    w_down = gaussian(seeds[2], (FF, D), FF ** -0.5, 0.0390625, ((0, 32), (1, 8)))
    grad_out = gaussian(seeds[3], (TOK, D), 1.0, 6.0, ((0, 32), (1, 8)))
    return dict(tokens_in=tokens_in, w_up=w_up, w_down=w_down, grad_out=grad_out)


def reference(tokens_in, w_up, w_down, grad_out):
    hidden = jnp.dot(tokens_in, w_up, preferred_element_type=jnp.float32)
    normal_cdf = 0.5 * (1.0 + lax.erf(hidden * 0.7071067811865476))
    activ = (hidden * normal_cdf).astype(jnp.bfloat16)
    output = jnp.dot(activ, w_down, preferred_element_type=jnp.float32).astype(jnp.bfloat16)
    grad_activ = jnp.dot(grad_out, w_down.T, preferred_element_type=jnp.float32)
    density = jnp.exp(-0.5 * hidden * hidden) * 0.3989422804014327
    grad_hidden = (grad_activ * (normal_cdf + hidden * density)).astype(jnp.bfloat16)
    token_scale = TOK ** -0.5
    grad_w_down = (jnp.dot(activ.T, grad_out, preferred_element_type=jnp.float32) * token_scale).astype(jnp.bfloat16)
    grad_w_up = (jnp.dot(tokens_in.T, grad_hidden, preferred_element_type=jnp.float32) * token_scale).astype(jnp.bfloat16)
    grad_tokens = jnp.dot(grad_hidden, w_up.T, preferred_element_type=jnp.float32).astype(jnp.bfloat16)
    return output, grad_tokens, grad_w_up, grad_w_down
```

```python
import jax
import jax.numpy as jnp
from jax import lax
from jax.sharding import PartitionSpec as P

ROWS = 8
SIDE = 4
ALL = ("row", "col", "rep")
XY = ("col", "rep")
TOP_POWER = 14.0
TINY = 1e-30
EXTRA = 8


def pairs(move):
    out = []
    for z in range(ROWS):
        for x in range(SIDE):
            for y in range(SIDE):
                for c in range(2):
                    tz, tx, ty, tc = move(z, x, y, c)
                    source = ((z * SIDE + x) * SIDE + y) * 2 + c
                    target = ((tz % ROWS * SIDE + tx % SIDE) * SIDE + ty % SIDE) * 2 + tc % 2
                    out.append((source, target))
    return out


def shift_row(array, step):
    return lax.ppermute(array, ALL, pairs(lambda z, x, y, c: (z + step, x, y, c)))


def shift_first(array, step):
    return lax.ppermute(
        array,
        ALL,
        pairs(lambda z, x, y, c: (z, x, y + step, c) if c == 0 else (z, x + step, y, c)),
    )


def shift_second(array, step):
    return lax.ppermute(
        array,
        ALL,
        pairs(lambda z, x, y, c: (z, x + step, y, c) if c == 0 else (z, x, y + step, c)),
    )


def swap_core(array, step=1):
    return lax.ppermute(array, ALL, pairs(lambda z, x, y, c: (z, x, y, c + step)))


def gather_tokens(own):
    line = jnp.concatenate([own] + [shift_first(own, -k) for k in (1, 2, 3)], axis=0)
    half = jnp.concatenate([line] + [shift_second(line, -j) for j in (1, 2, 3)], axis=0)
    return jnp.concatenate([half, swap_core(half)], axis=0)


def column_bound(array):
    return jnp.max(jnp.abs(array), axis=0, keepdims=True)


def send_scaled(array, bound, shift, step):
    rows, columns = array.shape
    power = jnp.ceil(jnp.log2(jnp.maximum(bound, TINY)))
    scaled = (array * jnp.exp2(TOP_POWER - power)).astype(jnp.float16)
    powers = jnp.broadcast_to(power.astype(jnp.float16), (EXTRA, columns))
    got = shift(jnp.concatenate([scaled, powers], axis=0), step)
    power = got[rows : rows + 1].astype(jnp.float32)
    return got[:rows].astype(jnp.float32) * jnp.exp2(power - TOP_POWER), jnp.exp2(power)


def scatter_tokens(partial):
    half = partial.shape[0] // 2
    bound = column_bound(partial)
    got, got_bound = send_scaled(partial[half:], bound, swap_core, 1)
    mine, bound = partial[:half] + got, bound + got_bound
    for shift in (shift_second, shift_first):
        part = mine.shape[0] // SIDE
        total, total_bound = mine[:part], bound
        for j in (1, 2, 3):
            got, got_bound = send_scaled(mine[j * part : (j + 1) * part], bound, shift, j)
            total, total_bound = total + got, total_bound + got_bound
        mine, bound = total, total_bound
    return mine.astype(jnp.bfloat16)


def scatter_row(partial, long_way):
    share = partial.shape[0] // ROWS
    at = lax.axis_index("row")
    own_bound = column_bound(partial)

    def chunk(offset):
        first = lax.rem(at + (offset + ROWS), ROWS) * share
        return lax.dynamic_slice_in_dim(partial, first, share, 0)

    total = chunk(0)
    for way, hops in ((long_way, ROWS // 2), (-long_way, ROWS // 2 - 1)):
        moving, bound = chunk(way * hops), own_bound
        for hop in range(hops, 0, -1):
            moving, bound = send_scaled(moving, bound, shift_row, way)
            if hop > 1:
                moving, bound = moving + chunk(way * (hop - 1)), bound + own_bound
        total = total + moving
    return total


def gather_row(own, long_way):
    found = {0: own}
    for way, hops in ((long_way, ROWS // 2), (-long_way, ROWS // 2 - 1)):
        moving = own
        for hop in range(1, hops + 1):
            moving = shift_row(moving, way)
            found[(-way * hop) % ROWS] = moving
    at = lax.axis_index("row")
    share = own.shape[0]
    whole = jnp.zeros((ROWS * share, own.shape[1]), own.dtype)
    for offset in range(ROWS):
        first = lax.rem(at + offset, ROWS) * share
        whole = lax.dynamic_update_slice_in_dim(whole, found[offset], first, 0)
    return whole


def gelu_parts(hidden):
    normal_cdf = 0.5 * (1.0 + lax.erf(hidden * 0.7071067811865476))
    density = jnp.exp(-0.5 * hidden * hidden) * 0.3989422804014327
    return (normal_cdf, density)


def on_device(tokens_in, w_up, w_down, grad_out):
    tokens_all = gather_tokens(tokens_in)
    token_scale = tokens_all.shape[0] ** (-0.5)
    hidden_part = jnp.dot(tokens_all, w_up, preferred_element_type=jnp.float32)
    grad_out_all = gather_tokens(grad_out)
    by_columns = (((1,), (1,)), ((), ()))
    by_rows = (((0,), (0,)), ((), ()))
    hidden = scatter_row(hidden_part, -1)
    grad_part = lax.dot_general(
        grad_out_all, w_down, by_columns, preferred_element_type=jnp.float32
    )
    normal_cdf, density = gelu_parts(hidden)
    activ = (hidden * normal_cdf).astype(jnp.bfloat16)
    grad_activ = scatter_row(grad_part, 1)
    grad_hidden = (grad_activ * (normal_cdf + hidden * density)).astype(jnp.bfloat16)
    activ_all = gather_row(activ, -1)
    output_part = jnp.dot(activ_all, w_down, preferred_element_type=jnp.float32)
    output = scatter_tokens(output_part)
    grad_all = gather_row(grad_hidden, 1)
    grad_tokens_part = lax.dot_general(grad_all, w_up, by_columns, preferred_element_type=jnp.float32)
    grad_tokens = scatter_tokens(grad_tokens_part)
    grad_w_down = (
        lax.dot_general(activ_all, grad_out_all, by_rows, preferred_element_type=jnp.float32)
        * token_scale
    ).astype(jnp.bfloat16)
    grad_w_up = (
        lax.dot_general(tokens_all, grad_all, by_rows, preferred_element_type=jnp.float32)
        * token_scale
    ).astype(jnp.bfloat16)
    return (output, grad_tokens, grad_w_up, grad_w_down)


def solution(mesh):
    return jax.shard_map(
        on_device,
        mesh=mesh,
        in_specs=(
            P(("col", "rep"), "row"),
            P("row", ("col", "rep")),
            P(("col", "rep"), "row"),
            P(("col", "rep"), "row"),
        ),
        out_specs=(
            P(("col", "rep"), "row"),
            P(("col", "rep"), "row"),
            P("row", ("col", "rep")),
            P(("col", "rep"), "row"),
        ),
        check_vma=False,
    )
```

```python
import jax
import jax.numpy as jnp
from jax import lax
from jax.sharding import PartitionSpec as P

ROWS = 8
SIDE = 4
ALL = ("row", "col", "rep")
XY = ("col", "rep")
TOP_POWER = 14.0
TINY = 1e-30
EXTRA = 8


def pairs(move):
    out = []
    for z in range(ROWS):
        for x in range(SIDE):
            for y in range(SIDE):
                for c in range(2):
                    tz, tx, ty, tc = move(z, x, y, c)
                    source = ((z * SIDE + x) * SIDE + y) * 2 + c
                    target = ((tz % ROWS * SIDE + tx % SIDE) * SIDE + ty % SIDE) * 2 + tc % 2
                    out.append((source, target))
    return out


def shift_row(array, step):
    return lax.ppermute(array, ALL, pairs(lambda z, x, y, c: (z + step, x, y, c)))


def exchange(array):
    side = range(SIDE)
    groups = [
        [(x * SIDE + y) * 2 for x in side for y in side],
        [(x * SIDE + y) * 2 + 1 for y in side for x in side],
    ]
    return lax.all_to_all(array, XY, 0, 0, axis_index_groups=groups, tiled=True)


def shift_major(array, step):
    return lax.ppermute(
        array,
        ALL,
        pairs(lambda z, x, y, c: (z, x, y + step, c) if c else (z, x + step, y, c)),
    )


def shift_minor(array, step):
    return lax.ppermute(
        array,
        ALL,
        pairs(lambda z, x, y, c: (z, x + step, y, c) if c else (z, x, y + step, c)),
    )


def place_in_plane():
    col, rep = lax.axis_index("col"), lax.axis_index("rep")
    x, y, core = col // 2, col % 2 * 2 + rep // 2, rep % 2
    return jnp.where(core == 0, x, y), jnp.where(core == 0, y, x)


def swap_core(array, step=1):
    return lax.ppermute(array, ALL, pairs(lambda z, x, y, c: (z, x, y, c + step)))


class Order:
    def __init__(self):
        self.last = None

    def take(self, arrays):
        if self.last is None:
            return arrays
        return lax.optimization_barrier((arrays, self.last))[0]

    def mark(self, arrays):
        self.last = arrays
        return arrays


def gather_chips(own):
    return exchange(
        jnp.broadcast_to(own[None], (SIDE * SIDE,) + own.shape).reshape(-1, own.shape[1])
    )


def column_bound(array):
    return jnp.max(jnp.abs(array), axis=0, keepdims=True)


def packed(array, bound):
    power = jnp.ceil(jnp.log2(jnp.maximum(bound, TINY)))
    scaled = (array * jnp.exp2(TOP_POWER - power)).astype(jnp.float16)
    powers = jnp.broadcast_to(power.astype(jnp.float16), (EXTRA, array.shape[1]))
    return jnp.concatenate([scaled, powers], axis=0)


def unpacked(got):
    rows = got.shape[0] - EXTRA
    power = got[rows : rows + 1].astype(jnp.float32)
    return got[:rows].astype(jnp.float32) * jnp.exp2(power - TOP_POWER), jnp.exp2(power)


class TokenScatter:
    def __init__(self, rows, product, order):
        half = rows.shape[0] // 2
        self.order = order
        sent = order.mark(product(rows[half:]).astype(jnp.bfloat16))
        self.got = [swap_core(sent)]
        self.rows, self.product = rows, product

    def add_own(self):
        rows = self.order.take(self.rows)
        self.mine = self.product(rows[: rows.shape[0] // 2])
        return self

    def start_line(self, at, shift):
        got = self.order.take(self.got)
        mine = self.mine
        for piece in got:
            mine = mine + piece.astype(jnp.float32)
        share = mine.shape[0] // SIDE

        def chunk(offset):
            first = lax.rem(at + offset, SIDE) * share
            return lax.dynamic_slice_in_dim(mine, first, share, 0)

        sent = self.order.mark([chunk(step).astype(jnp.bfloat16) for step in (1, 2, 3)])
        self.got = [shift(piece, step) for step, piece in zip((1, 2, 3), sent)]
        self.mine = chunk(0)

    def end_line(self):
        mine = self.mine
        for piece in self.order.take(self.got):
            mine = mine + piece.astype(jnp.float32)
        return self.order.mark(mine.astype(jnp.bfloat16))


class RowScatter:
    def __init__(self, partial, long_way, order):
        self.partial, self.order = partial, order
        self.bound = column_bound(partial)
        self.left = {long_way: ROWS // 2, -long_way: ROWS // 2 - 1}
        self.got = {}
        self.total = self.chunk(0)

    def chunk(self, offset):
        share = self.partial.shape[0] // ROWS
        first = lax.rem(lax.axis_index("row") + (offset + ROWS), ROWS) * share
        return lax.dynamic_slice_in_dim(self.partial, first, share, 0)

    def hop(self):
        got = self.order.take(self.got)
        payloads = {}
        for way, left in self.left.items():
            if left == 0:
                self.total = self.total + unpacked(got[way])[0]
                continue
            moving, bound = self.chunk(way * left), self.bound
            if way in got:
                values, got_bound = unpacked(got[way])
                moving, bound = moving + values, bound + got_bound
            payloads[way] = packed(moving, bound)
        self.got = {}
        for way, payload in self.order.mark(payloads).items():
            self.got[way] = shift_row(payload, way)
            self.left[way] -= 1

    def end(self):
        for payload in self.order.take(self.got).values():
            self.total = self.total + unpacked(payload)[0]
        return self.total


class RowGather:
    def __init__(self, own, long_way, order):
        self.own, self.order = own, order
        self.found = {0: own}
        self.hops = {long_way: ROWS // 2, -long_way: ROWS // 2 - 1}
        self.moving = {way: own for way in self.hops}
        self.done = 0

    def hop(self):
        self.done += 1
        moving = self.order.mark(self.order.take(self.moving))
        self.keep(moving)
        self.moving = {}
        for way, hops in self.hops.items():
            if self.done <= hops:
                self.moving[way] = shift_row(moving[way], way)

    def keep(self, moving):
        for way, piece in moving.items():
            self.found[(-way * (self.done - 1)) % ROWS] = piece

    def whole(self):
        self.done += 1
        self.keep(self.order.take(self.moving))
        at = lax.axis_index("row")
        share = self.own.shape[0]
        whole = jnp.zeros((ROWS * share, self.own.shape[1]), self.own.dtype)
        for offset in range(ROWS):
            first = lax.rem(at + offset, ROWS) * share
            whole = lax.dynamic_update_slice_in_dim(whole, self.found[offset], first, 0)
        return whole


def gelu_parts(hidden):
    normal_cdf = 0.5 * (1.0 + lax.erf(hidden * 0.7071067811865476))
    density = jnp.exp(-0.5 * hidden * hidden) * 0.3989422804014327
    return (normal_cdf, density)


def on_device(tokens_in, w_up, w_down, grad_out):
    by_columns = (((1,), (1,)), ((), ()))
    by_rows = (((0,), (0,)), ((), ()))
    order = Order()

    def up_product(rows):
        return jnp.dot(rows, w_up, preferred_element_type=jnp.float32)

    def up_back(rows):
        return lax.dot_general(rows, w_up, by_columns, preferred_element_type=jnp.float32)

    def down_product(rows):
        return jnp.dot(rows, w_down, preferred_element_type=jnp.float32)

    def down_back(rows):
        return lax.dot_general(rows, w_down, by_columns, preferred_element_type=jnp.float32)

    def weight_grad(left, right):
        total = lax.dot_general(left, right, by_rows, preferred_element_type=jnp.float32)
        return order.mark((total * left.shape[0] ** (-0.5)).astype(jnp.bfloat16))

    tokens_own = order.mark(gather_chips(tokens_in))
    grad_own = gather_chips(order.take(grad_out))
    tokens_other = swap_core(tokens_own)
    hidden_part = jnp.concatenate([up_product(tokens_own), up_product(tokens_other)], axis=0)
    up = RowScatter(hidden_part, -1, order)
    up.hop()
    up.hop()
    grad_own = order.mark(order.take(grad_own))
    grad_other = swap_core(grad_own)
    grad_other = order.take(grad_other)
    grad_part = jnp.concatenate([down_back(grad_own), down_back(grad_other)], axis=0)
    down = RowScatter(grad_part, 1, order)
    down.hop()
    up.hop()
    down.hop()
    up.hop()
    down.hop()
    hidden = up.end()
    normal_cdf, density = gelu_parts(hidden)
    activ = order.mark((hidden * normal_cdf).astype(jnp.bfloat16))
    gelu_slope = normal_cdf + hidden * density
    activ_rows = RowGather(activ, -1, order)
    activ_rows.hop()
    down.hop()
    activ_rows.hop()
    grad_hidden = order.mark((down.end() * gelu_slope).astype(jnp.bfloat16))
    grad_rows = RowGather(grad_hidden, 1, order)
    grad_rows.hop()
    activ_rows.hop()
    grad_rows.hop()
    activ_rows.hop()
    grad_rows.hop()
    activ_all = activ_rows.whole()
    output = TokenScatter(activ_all, down_product, order).add_own()
    major, minor = place_in_plane()
    output.start_line(major, shift_major)
    grad_rows.hop()
    grad_out_all = jnp.concatenate(order.take([grad_own, grad_other]), axis=0)
    grad_w_down = weight_grad(order.take(activ_all), grad_out_all)
    grad_all = grad_rows.whole()
    grad_tokens = TokenScatter(grad_all, up_back, order).add_own()
    grad_tokens.start_line(major, shift_major)
    output.start_line(minor, shift_minor)
    tokens_all = jnp.concatenate(order.take([tokens_own, tokens_other]), axis=0)
    grad_w_up = weight_grad(tokens_all, order.take(grad_all))
    grad_tokens.start_line(minor, shift_minor)
    output = output.end_line()
    grad_tokens = grad_tokens.end_line()
    return (output, grad_tokens, grad_w_up, grad_w_down)


def solution(mesh):
    return jax.shard_map(
        on_device,
        mesh=mesh,
        in_specs=(
            P(("col", "rep"), "row"),
            P("row", ("col", "rep")),
            P(("col", "rep"), "row"),
            P(("col", "rep"), "row"),
        ),
        out_specs=(
            P(("col", "rep"), "row"),
            P(("col", "rep"), "row"),
            P("row", ("col", "rep")),
            P(("col", "rep"), "row"),
        ),
        check_vma=False,
    )
```

```python
import jax
import jax.numpy as jnp
from jax import lax
from jax.sharding import PartitionSpec as P

ROWS = 8
SIDE = 4
ALL = ("row", "col", "rep")
XY = ("col", "rep")
TOP_POWER = 14.0
TINY = 1e-30
EXTRA = 8


def pairs(move):
    out = []
    for z in range(ROWS):
        for x in range(SIDE):
            for y in range(SIDE):
                for c in range(2):
                    tz, tx, ty, tc = move(z, x, y, c)
                    source = ((z * SIDE + x) * SIDE + y) * 2 + c
                    target = ((tz % ROWS * SIDE + tx % SIDE) * SIDE + ty % SIDE) * 2 + tc % 2
                    out.append((source, target))
    return out


def shift_row(array, step):
    return lax.ppermute(array, ALL, pairs(lambda z, x, y, c: (z + step, x, y, c)))


def exchange(array):
    side = range(SIDE)
    groups = [
        [(x * SIDE + y) * 2 for x in side for y in side],
        [(x * SIDE + y) * 2 + 1 for y in side for x in side],
    ]
    return lax.all_to_all(array, XY, 0, 0, axis_index_groups=groups, tiled=True)


def shift_major(array, step):
    return lax.ppermute(
        array,
        ALL,
        pairs(lambda z, x, y, c: (z, x, y + step, c) if c else (z, x + step, y, c)),
    )


def shift_minor(array, step):
    return lax.ppermute(
        array,
        ALL,
        pairs(lambda z, x, y, c: (z, x + step, y, c) if c else (z, x, y + step, c)),
    )


def place_in_plane():
    col, rep = lax.axis_index("col"), lax.axis_index("rep")
    x, y, core = col // 2, col % 2 * 2 + rep // 2, rep % 2
    return jnp.where(core == 0, x, y), jnp.where(core == 0, y, x)


def swap_core(array, step=1):
    return lax.ppermute(array, ALL, pairs(lambda z, x, y, c: (z, x, y, c + step)))


class Order:
    def __init__(self):
        self.last = None

    def take(self, arrays):
        if self.last is None:
            return arrays
        return lax.optimization_barrier((arrays, self.last))[0]

    def mark(self, arrays):
        self.last = arrays
        return arrays


def gather_chips(own):
    return exchange(
        jnp.broadcast_to(own[None], (SIDE * SIDE,) + own.shape).reshape(-1, own.shape[1])
    )


def column_bound(array):
    return jnp.max(jnp.abs(array), axis=0, keepdims=True)


def packed(array, bound):
    power = jnp.ceil(jnp.log2(jnp.maximum(bound, TINY)))
    scaled = (array * jnp.exp2(TOP_POWER - power)).astype(jnp.float16)
    powers = jnp.broadcast_to(power.astype(jnp.float16), (EXTRA, array.shape[1]))
    return jnp.concatenate([scaled, powers], axis=0)


def unpacked(got):
    rows = got.shape[0] - EXTRA
    power = got[rows : rows + 1].astype(jnp.float32)
    return got[:rows].astype(jnp.float32) * jnp.exp2(power - TOP_POWER), jnp.exp2(power)


class TokenScatter:
    def __init__(self, rows, product, order):
        half = rows.shape[0] // 2
        self.order = order
        sent = order.mark(product(rows[half:]).astype(jnp.bfloat16))
        self.got = [swap_core(sent)]
        self.rows, self.product = rows, product

    def add_own(self):
        rows = self.order.take(self.rows)
        self.mine = self.product(rows[: rows.shape[0] // 2])
        return self

    def start_line(self, at, shift):
        got = self.order.take(self.got)
        mine = self.mine
        for piece in got:
            mine = mine + piece.astype(jnp.float32)
        share = mine.shape[0] // SIDE

        def chunk(offset):
            first = lax.rem(at + offset, SIDE) * share
            return lax.dynamic_slice_in_dim(mine, first, share, 0)

        sent = self.order.mark([chunk(step).astype(jnp.bfloat16) for step in (1, 2, 3)])
        self.got = [shift(piece, step) for step, piece in zip((1, 2, 3), sent)]
        self.mine = chunk(0)

    def line_total(self):
        mine = self.mine
        for piece in self.order.take(self.got):
            mine = mine + piece.astype(jnp.float32)
        return self.order.mark(mine)


def last_line(totals, at, order):
    share = totals[0].shape[0] // SIDE

    def chunk(total, offset):
        start = lax.rem(at + offset, SIDE) * share
        return lax.dynamic_slice_in_dim(total, start, share, 0)

    sent = order.mark(
        [
            jnp.concatenate([chunk(total, step).astype(jnp.bfloat16) for total in totals], axis=0)
            for step in (1, 2, 3)
        ]
    )
    got = [shift_minor(piece, step) for step, piece in zip((1, 2, 3), sent)]
    return totals, chunk, share, got


def end_lines(totals, chunk, share, got, order):
    got = order.take(got)
    results = []
    for place, total in enumerate(totals):
        mine = chunk(total, 0)
        for piece in got:
            mine = mine + piece[place * share : (place + 1) * share].astype(jnp.float32)
        results.append(mine.astype(jnp.bfloat16))
    return results


class RowScatter:
    def __init__(self, partial, long_way, order):
        self.partial, self.order = partial, order
        self.bound = column_bound(partial)
        self.left = {long_way: ROWS // 2, -long_way: ROWS // 2 - 1}
        self.got = {}
        self.total = self.chunk(0)

    def chunk(self, offset):
        share = self.partial.shape[0] // ROWS
        first = lax.rem(lax.axis_index("row") + (offset + ROWS), ROWS) * share
        return lax.dynamic_slice_in_dim(self.partial, first, share, 0)

    def hop(self):
        got = self.order.take(self.got)
        payloads = {}
        for way, left in self.left.items():
            if left == 0:
                self.total = self.total + unpacked(got[way])[0]
                continue
            moving, bound = self.chunk(way * left), self.bound
            if way in got:
                values, got_bound = unpacked(got[way])
                moving, bound = moving + values, bound + got_bound
            payloads[way] = packed(moving, bound)
        self.got = {}
        for way, payload in self.order.mark(payloads).items():
            self.got[way] = shift_row(payload, way)
            self.left[way] -= 1

    def end(self):
        for payload in self.order.take(self.got).values():
            self.total = self.total + unpacked(payload)[0]
        return self.total


class RowGather:
    def __init__(self, own, long_way, order):
        self.own, self.order = own, order
        self.found = {0: own}
        self.hops = {long_way: ROWS // 2, -long_way: ROWS // 2 - 1}
        self.moving = {way: own for way in self.hops}
        self.done = 0

    def hop(self):
        self.done += 1
        moving = self.order.mark(self.order.take(self.moving))
        self.keep(moving)
        self.moving = {}
        for way, hops in self.hops.items():
            if self.done <= hops:
                self.moving[way] = shift_row(moving[way], way)

    def keep(self, moving):
        for way, piece in moving.items():
            self.found[(-way * (self.done - 1)) % ROWS] = piece

    def whole(self):
        self.done += 1
        self.keep(self.order.take(self.moving))
        at = lax.axis_index("row")
        share = self.own.shape[0]
        whole = jnp.zeros((ROWS * share, self.own.shape[1]), self.own.dtype)
        for offset in range(ROWS):
            first = lax.rem(at + offset, ROWS) * share
            whole = lax.dynamic_update_slice_in_dim(whole, self.found[offset], first, 0)
        return whole


def gelu_parts(hidden):
    normal_cdf = 0.5 * (1.0 + lax.erf(hidden * 0.7071067811865476))
    density = jnp.exp(-0.5 * hidden * hidden) * 0.3989422804014327
    return (normal_cdf, density)


def on_device(tokens_in, w_up, w_down, grad_out):
    by_columns = (((1,), (1,)), ((), ()))
    by_rows = (((0,), (0,)), ((), ()))
    order = Order()

    def up_product(rows):
        return jnp.dot(rows, w_up, preferred_element_type=jnp.float32)

    def up_back(rows):
        return lax.dot_general(rows, w_up, by_columns, preferred_element_type=jnp.float32)

    def down_product(rows):
        return jnp.dot(rows, w_down, preferred_element_type=jnp.float32)

    def down_back(rows):
        return lax.dot_general(rows, w_down, by_columns, preferred_element_type=jnp.float32)

    def weight_grad(left, right):
        total = lax.dot_general(left, right, by_rows, preferred_element_type=jnp.float32)
        return order.mark((total * left.shape[0] ** (-0.5)).astype(jnp.bfloat16))

    tokens_own = order.mark(gather_chips(tokens_in))
    grad_own = gather_chips(order.take(grad_out))
    tokens_other = swap_core(tokens_own)
    hidden_part = jnp.concatenate([up_product(tokens_own), up_product(tokens_other)], axis=0)
    up = RowScatter(hidden_part, -1, order)
    up.hop()
    tokens_all = order.mark(jnp.concatenate(order.take([tokens_own, tokens_other]), axis=0))
    up.hop()
    grad_own = order.mark(order.take(grad_own))
    grad_other = swap_core(grad_own)
    grad_other = order.take(grad_other)
    grad_part = jnp.concatenate([down_back(grad_own), down_back(grad_other)], axis=0)
    down = RowScatter(grad_part, 1, order)
    down.hop()
    up.hop()
    down.hop()
    up.hop()
    down.hop()
    hidden = up.end()
    normal_cdf, density = gelu_parts(hidden)
    activ = order.mark((hidden * normal_cdf).astype(jnp.bfloat16))
    gelu_slope = normal_cdf + hidden * density
    activ_rows = RowGather(activ, -1, order)
    activ_rows.hop()
    down.hop()
    grad_out_all = order.mark(jnp.concatenate(order.take([grad_own, grad_other]), axis=0))
    grad_hidden = order.mark((down.end() * gelu_slope).astype(jnp.bfloat16))
    grad_rows = RowGather(grad_hidden, 1, order)
    grad_rows.hop()
    activ_rows.hop()
    grad_rows.hop()
    activ_rows.hop()
    grad_rows.hop()
    activ_rows.hop()
    grad_rows.hop()
    activ_all = activ_rows.whole()
    output = TokenScatter(activ_all, down_product, order).add_own()
    major, minor = place_in_plane()
    output.start_line(major, shift_major)
    grad_all = grad_rows.whole()
    grad_tokens = TokenScatter(grad_all, up_back, order).add_own()
    grad_tokens.start_line(major, shift_major)
    grad_w_up = weight_grad(tokens_all, order.take(grad_all))
    lines = last_line([output.line_total(), grad_tokens.line_total()], minor, order)
    grad_w_down = weight_grad(order.take(activ_all), grad_out_all)
    output, grad_tokens = end_lines(*lines, order)
    return (output, grad_tokens, grad_w_up, grad_w_down)


def solution(mesh):
    return jax.shard_map(
        on_device,
        mesh=mesh,
        in_specs=(
            P(("col", "rep"), "row"),
            P("row", ("col", "rep")),
            P(("col", "rep"), "row"),
            P(("col", "rep"), "row"),
        ),
        out_specs=(
            P(("col", "rep"), "row"),
            P(("col", "rep"), "row"),
            P("row", ("col", "rep")),
            P(("col", "rep"), "row"),
        ),
        check_vma=False,
    )
```

```python
import jax
import jax.numpy as jnp
from jax import lax
from jax.sharding import PartitionSpec as P

ROWS = 8
SIDE = 4
ALL = ("row", "col", "rep")
XY = ("col", "rep")
TOP_POWER = 14.0
TINY = 1e-30
EXTRA = 8


def pairs(move):
    out = []
    for z in range(ROWS):
        for x in range(SIDE):
            for y in range(SIDE):
                for c in range(2):
                    tz, tx, ty, tc = move(z, x, y, c)
                    source = ((z * SIDE + x) * SIDE + y) * 2 + c
                    target = ((tz % ROWS * SIDE + tx % SIDE) * SIDE + ty % SIDE) * 2 + tc % 2
                    out.append((source, target))
    return out


def shift_row(array, step):
    return lax.ppermute(array, ALL, pairs(lambda z, x, y, c: (z + step, x, y, c)))


def exchange(array):
    side = range(SIDE)
    groups = [
        [(x * SIDE + y) * 2 for x in side for y in side],
        [(x * SIDE + y) * 2 + 1 for y in side for x in side],
    ]
    return lax.all_to_all(array, XY, 0, 0, axis_index_groups=groups, tiled=True)


def shift_major(array, step):
    return lax.ppermute(
        array,
        ALL,
        pairs(lambda z, x, y, c: (z, x, y + step, c) if c else (z, x + step, y, c)),
    )


def shift_minor(array, step):
    return lax.ppermute(
        array,
        ALL,
        pairs(lambda z, x, y, c: (z, x + step, y, c) if c else (z, x, y + step, c)),
    )


def place_in_plane():
    col, rep = lax.axis_index("col"), lax.axis_index("rep")
    x, y, core = col // 2, col % 2 * 2 + rep // 2, rep % 2
    return jnp.where(core == 0, x, y), jnp.where(core == 0, y, x)


def swap_core(array, step=1):
    return lax.ppermute(array, ALL, pairs(lambda z, x, y, c: (z, x, y, c + step)))


class Order:
    def __init__(self):
        self.last = None

    def take(self, arrays):
        if self.last is None:
            return arrays
        return lax.optimization_barrier((arrays, self.last))[0]

    def mark(self, arrays):
        self.last = arrays
        return arrays


def gather_chips(own):
    return exchange(
        jnp.broadcast_to(own[None], (SIDE * SIDE,) + own.shape).reshape(-1, own.shape[1])
    )


def column_bound(array):
    return jnp.max(jnp.abs(array), axis=0, keepdims=True)


def packed(array, bound):
    power = jnp.ceil(jnp.log2(jnp.maximum(bound, TINY)))
    scaled = (array * jnp.exp2(TOP_POWER - power)).astype(jnp.float16)
    powers = jnp.broadcast_to(power.astype(jnp.float16), (EXTRA, array.shape[1]))
    return jnp.concatenate([scaled, powers], axis=0)


def unpacked(got):
    rows = got.shape[0] - EXTRA
    power = got[rows : rows + 1].astype(jnp.float32)
    return got[:rows].astype(jnp.float32) * jnp.exp2(power - TOP_POWER), jnp.exp2(power)


class TokenScatter:
    def __init__(self, rows, product, order):
        half = rows.shape[0] // 2
        self.order = order
        sent = order.mark(product(rows[half:]).astype(jnp.bfloat16))
        self.got = [swap_core(sent)]
        self.rows, self.product = rows, product

    def add_own(self):
        rows = self.order.take(self.rows)
        self.mine = self.product(rows[: rows.shape[0] // 2])
        return self

    def start_line(self, at, shift):
        got = self.order.take(self.got)
        mine = self.mine
        for piece in got:
            mine = mine + piece.astype(jnp.float32)
        share = mine.shape[0] // SIDE

        def chunk(offset):
            first = lax.rem(at + offset, SIDE) * share
            return lax.dynamic_slice_in_dim(mine, first, share, 0)

        sent = self.order.mark([chunk(step).astype(jnp.bfloat16) for step in (1, 2, 3)])
        self.got = [shift(piece, step) for step, piece in zip((1, 2, 3), sent)]
        self.mine = chunk(0)

    def end_line(self):
        mine = self.mine
        for piece in self.order.take(self.got):
            mine = mine + piece.astype(jnp.float32)
        return self.order.mark(mine.astype(jnp.bfloat16))


class RowScatter:
    def __init__(self, partial, long_way, order):
        self.partial, self.order = partial, order
        self.bound = column_bound(partial)
        self.left = {long_way: ROWS // 2, -long_way: ROWS // 2 - 1}
        self.got = {}
        self.total = self.chunk(0)

    def chunk(self, offset):
        share = self.partial.shape[0] // ROWS
        first = lax.rem(lax.axis_index("row") + (offset + ROWS), ROWS) * share
        return lax.dynamic_slice_in_dim(self.partial, first, share, 0)

    def hop(self):
        got = self.order.take(self.got)
        payloads = {}
        for way, left in self.left.items():
            if left == 0:
                self.total = self.total + unpacked(got[way])[0]
                continue
            moving, bound = self.chunk(way * left), self.bound
            if way in got:
                values, got_bound = unpacked(got[way])
                moving, bound = moving + values, bound + got_bound
            payloads[way] = packed(moving, bound)
        self.got = {}
        for way, payload in self.order.mark(payloads).items():
            self.got[way] = shift_row(payload, way)
            self.left[way] -= 1

    def end(self):
        for payload in self.order.take(self.got).values():
            self.total = self.total + unpacked(payload)[0]
        return self.total


class RowGather:
    def __init__(self, own, long_way, order):
        self.own, self.order = own, order
        self.found = {0: own}
        self.hops = {long_way: ROWS // 2, -long_way: ROWS // 2 - 1}
        self.moving = {way: own for way in self.hops}
        self.done = 0

    def hop(self):
        self.done += 1
        moving = self.order.mark(self.order.take(self.moving))
        self.keep(moving)
        self.moving = {}
        for way, hops in self.hops.items():
            if self.done <= hops:
                self.moving[way] = shift_row(moving[way], way)

    def keep(self, moving):
        for way, piece in moving.items():
            self.found[(-way * (self.done - 1)) % ROWS] = piece

    def whole(self):
        self.done += 1
        self.keep(self.order.take(self.moving))
        at = lax.axis_index("row")
        share = self.own.shape[0]
        whole = jnp.zeros((ROWS * share, self.own.shape[1]), self.own.dtype)
        for offset in range(ROWS):
            first = lax.rem(at + offset, ROWS) * share
            whole = lax.dynamic_update_slice_in_dim(whole, self.found[offset], first, 0)
        return whole


def gelu_parts(hidden):
    normal_cdf = 0.5 * (1.0 + lax.erf(hidden * 0.7071067811865476))
    density = jnp.exp(-0.5 * hidden * hidden) * 0.3989422804014327
    return (normal_cdf, density)


def on_device(tokens_in, w_up, w_down, grad_out):
    by_columns = (((1,), (1,)), ((), ()))
    by_rows = (((0,), (0,)), ((), ()))
    order = Order()

    def up_product(rows):
        return jnp.dot(rows, w_up, preferred_element_type=jnp.float32)

    def up_back(rows):
        return lax.dot_general(rows, w_up, by_columns, preferred_element_type=jnp.float32)

    def down_product(rows):
        return jnp.dot(rows, w_down, preferred_element_type=jnp.float32)

    def down_back(rows):
        return lax.dot_general(rows, w_down, by_columns, preferred_element_type=jnp.float32)

    def weight_grad(left, right):
        total = lax.dot_general(left, right, by_rows, preferred_element_type=jnp.float32)
        return order.mark((total * left.shape[0] ** (-0.5)).astype(jnp.bfloat16))

    tokens_own = order.mark(gather_chips(tokens_in))
    grad_own = gather_chips(order.take(grad_out))
    tokens_other = swap_core(tokens_own)
    hidden_part = jnp.concatenate([up_product(tokens_own), up_product(tokens_other)], axis=0)
    up = RowScatter(hidden_part, -1, order)
    up.hop()
    tokens_all = order.mark(jnp.concatenate(order.take([tokens_own, tokens_other]), axis=0))
    up.hop()
    grad_own = order.mark(order.take(grad_own))
    grad_other = swap_core(grad_own)
    grad_other = order.take(grad_other)
    grad_part = jnp.concatenate([down_back(grad_own), down_back(grad_other)], axis=0)
    down = RowScatter(grad_part, 1, order)
    down.hop()
    up.hop()
    down.hop()
    up.hop()
    down.hop()
    hidden = up.end()
    normal_cdf, density = gelu_parts(hidden)
    activ = order.mark((hidden * normal_cdf).astype(jnp.bfloat16))
    gelu_slope = normal_cdf + hidden * density
    activ_rows = RowGather(activ, -1, order)
    activ_rows.hop()
    down.hop()
    activ_rows.hop()
    grad_hidden = order.mark((down.end() * gelu_slope).astype(jnp.bfloat16))
    grad_rows = RowGather(grad_hidden, 1, order)
    grad_rows.hop()
    activ_rows.hop()
    grad_rows.hop()
    activ_rows.hop()
    grad_rows.hop()
    activ_all = activ_rows.whole()
    output = TokenScatter(activ_all, down_product, order).add_own()
    major, minor = place_in_plane()
    output.start_line(major, shift_major)
    grad_rows.hop()
    grad_out_all = jnp.concatenate(order.take([grad_own, grad_other]), axis=0)
    grad_w_down = weight_grad(order.take(activ_all), grad_out_all)
    grad_all = grad_rows.whole()
    grad_tokens = TokenScatter(grad_all, up_back, order).add_own()
    grad_tokens.start_line(major, shift_major)
    output.start_line(minor, shift_minor)
    grad_w_up = weight_grad(tokens_all, order.take(grad_all))
    grad_tokens.start_line(minor, shift_minor)
    output = output.end_line()
    grad_tokens = grad_tokens.end_line()
    return (output, grad_tokens, grad_w_up, grad_w_down)


def solution(mesh):
    return jax.shard_map(
        on_device,
        mesh=mesh,
        in_specs=(
            P(("col", "rep"), "row"),
            P("row", ("col", "rep")),
            P(("col", "rep"), "row"),
            P(("col", "rep"), "row"),
        ),
        out_specs=(
            P(("col", "rep"), "row"),
            P(("col", "rep"), "row"),
            P("row", ("col", "rep")),
            P(("col", "rep"), "row"),
        ),
        check_vma=False,
    )
```
